512 devices in a mesh: replica: 64 (over x, y, z_hi), fsdp: 8 (over z_lo, core).
Axes of the slice: x: 4, y: 8, z: 8 (z_hi: 2, z_lo: 4; z = z_hi * 4 + z_lo), core: 2. Of those that a mesh axis runs over, the one named last changes fastest.
Arguments:
- partner: int32 [64], replicated, may hold values from 0 to 63, as said below
- pseudo_grad: bfloat16 [64, 4096, 512], P('replica', 'fsdp'), may hold values from -6 to 6
- momentum: bfloat16 [64, 4096, 512], P('replica', 'fsdp'), may hold values from -4 to 4
- outer_params: bfloat16 [64, 4096, 512], P('replica', 'fsdp'), may hold values from -6 to 6
- activations: bfloat16 [64, 1024, 4096], P('replica', 'fsdp'), may hold values from -6 to 6
- norm_gain: float32 [64, 4096], P('replica'), may hold values from 0.1 to 1.9
- key_weight: bfloat16 [64, 4096, 512], P('replica', 'fsdp'), may hold values from -0.09375 to 0.09375
- key_cotangent: bfloat16 [64, 1024, 512], P('replica', 'fsdp'), may hold values from -6 to 6
Outputs:
- new_params: bfloat16 [64, 4096, 512], P('replica', 'fsdp')
- new_momentum: bfloat16 [64, 4096, 512], P('replica', 'fsdp')
- keys: bfloat16 [64, 1024, 512], P('replica', 'fsdp')
- weight_grad: bfloat16 [64, 4096, 512], P('replica', 'fsdp')
- gain_grad: float32 [64, 4096], P('replica')
The draws below stay inside these ranges and needn't reach their ends.
Inputs may be any that keep to these rules, and one draw needn't show every extreme that they name: partner[partner[r]] == r and partner[r] != r for every replica r: the replicas form 64 / 2 disjoint pairs.
All inputs are finite; a program needn't handle non-finite values.
Results may differ from the reference program's by a relative error of at most 0.017.
Values may be sent and summed in bfloat16 or wider, within the bound.
A program may use at most 64 MiB of HBM per device.

```python
import jax
import jax.numpy as jnp
from jax import lax

D = 4096
TOK_DEV = 128
KC = 512
REPS = 64
TOKENS = 1024
N_FSDP = 8


def draw_partner(key, part):
    key = jax.random.fold_in(key, 7)
    order = jax.random.permutation(key, REPS).astype(jnp.int32)
    first_half = order[0::2]
    second_half = order[1::2]
    result = jnp.zeros((REPS,), jnp.int32)
    result = result.at[first_half].set(second_half)
    result = result.at[second_half].set(first_half)
    return result


def steps_of(own_key, dims, pieces, low, top_value):
    def one(axis_at, blocks):
        heights = jax.random.uniform(jax.random.fold_in(jax.random.fold_in(own_key, 6), axis_at), (blocks,), jnp.float32, low / len(pieces), top_value / len(pieces))
        return jnp.repeat(jnp.exp(heights), dims[axis_at] // blocks).reshape((-1,) + (1,) * (len(dims) - axis_at - 1))

    level = one(*pieces[0])
    for cut in pieces[1:]:
        level = level * one(*cut)
    return level


def scatter_about(key, shape, spread, bound, pieces=(), dtype=jnp.bfloat16):
    array = spread * jax.random.normal(key, shape, jnp.float32)
    if pieces:
        array = array * steps_of(key, shape, pieces, -0.22, 0.18)
    return jnp.clip(array, -bound, bound).astype(dtype)


def setup_inputs(seed: int = 0) -> dict:
    keys = jax.random.split(jax.random.key(seed), 9)
    return {
        "partner": draw_partner(jax.random.fold_in(keys[8], 71), 0),
        "pseudo_grad": scatter_about(keys[1], (REPS, D, KC), 1.0, 6.0, ((0, 64), (1, 8))),
        "momentum": scatter_about(keys[2], (REPS, D, KC), 0.5, 4.0, ((0, 64), (1, 8))),
        "outer_params": scatter_about(keys[3], (REPS, D, KC), 1.0, 6.0, ((0, 64), (1, 8))),
        "activations": scatter_about(keys[4], (REPS, TOKENS, D), 1.0, 6.0, ((0, 64), (1, 8))),
        "norm_gain": jnp.clip(1.0 + 0.18 * jax.random.normal(keys[5], (REPS, D), jnp.float32), 0.1, 1.9),
        "key_weight": scatter_about(keys[6], (REPS, D, KC), D ** -0.5, 0.09375, ((0, 64), (1, 8))),
        "key_cotangent": scatter_about(keys[7], (REPS, TOKENS, KC), 1.0, 6.0, ((0, 64), (1, 8))),
    }


MOMENT_RATE = 0.9
OUTER_RATE = 0.7
NORM_EPS = 1e-05

def one_replica(items):
    acts, gain, weight, cotangent = items
    wide_acts = acts.astype(jnp.float32)
    inv_rms = lax.rsqrt(lax.optimization_barrier(jnp.mean(wide_acts * wide_acts, axis=-1, keepdims=True)) + NORM_EPS)
    normed = (wide_acts * inv_rms * gain).astype(jnp.bfloat16)
    normed_wide = normed.astype(jnp.float32)
    weight_wide = weight.astype(jnp.float32)
    cot_wide = cotangent.astype(jnp.float32)
    key_out = jnp.dot(normed_wide, weight_wide).astype(jnp.bfloat16)
    block_normed = normed_wide.reshape(N_FSDP, TOK_DEV, D)
    block_cot = cot_wide.reshape(N_FSDP, TOK_DEV, KC)
    partial_sums = jnp.einsum('std,stk->sdk', block_normed, block_cot)
    rounded = lax.optimization_barrier(partial_sums.astype(jnp.bfloat16)).astype(jnp.float32)
    grad_out = lax.optimization_barrier(jnp.sum(rounded, axis=0)).astype(jnp.bfloat16)
    normed_grad = jnp.dot(cot_wide, weight_wide.T)
    gain_out = lax.optimization_barrier(jnp.sum(normed_grad * wide_acts * inv_rms, axis=0))
    return (key_out, grad_out, gain_out)

def reference(partner, pseudo_grad, momentum, outer_params, activations, norm_gain, key_weight, key_cotangent):
    own_grad = pseudo_grad.astype(jnp.float32)
    other_grad = jnp.take(own_grad, partner.astype(jnp.int32), axis=0)
    pair_mean = (own_grad + other_grad) * 0.5
    moment = MOMENT_RATE * momentum.astype(jnp.float32) + pair_mean
    fresh = outer_params.astype(jnp.float32) - OUTER_RATE * (pair_mean + MOMENT_RATE * moment)
    key_out, grad_out, gain_out = lax.map(one_replica, (activations, norm_gain, key_weight, key_cotangent))
    return (fresh.astype(jnp.bfloat16), moment.astype(jnp.bfloat16), key_out, grad_out, gain_out)
```

```python
import jax
import jax.numpy as jnp
from jax import lax
from jax.experimental import pallas as pl
from jax.experimental.pallas import tpu as pltpu
from jax.sharding import PartitionSpec as P

MOMENT_RATE = 0.9
OUTER_RATE = 0.7
NORM_EPS = 1e-05

MESH = pl.DeviceIdType.MESH
NX, NY = 4, 8
NQ = NX * NY
NP = 4
NF = 2 * NP
TOK = 128
D = 4096
BLK = D // NF
KC = 512
CUTS = 2
CW = KC // CUTS
ROWS = BLK // NQ

bf16 = jnp.bfloat16
f32 = jnp.float32


def body_kernel(
    partner, grad_h, mom_h, par_h, act_h, gain_v, w_h, cot_h,
    fresh_h, moment_h, keys_h, wgrad_h, ggrad_h,
    grad_v, mom_v, par_v, act_v, w_v, cot_v,
    met, back, mirror,
    acts, cots, x_in, x_out, u_in, u_out, d_in, d_out, own_part,
    wide_w, gcol, keys_v, wgrad_v, ggrad_v, fresh_v, moment_v, rms_v,
    load_sem, out_sem, one_send, one_recv, z_send, z_recv, two_send, two_recv,
    act_send, act_recv, cu_send, cd_send, cx_send, c_recv,
    x_send, x_recv, u_send, u_recv, d_send, d_recv, g_send, g_recv,
):
    r = lax.axis_index("replica")
    f = lax.axis_index("fsdp")
    q = r // 2
    half = r % 2
    qx, qy = q // NY, q % NY
    p = f // 2
    c = f % 2

    def at(chip, core):
        return (r, chip * 2 + core)

    def peer(k):
        px = (qx + k // NY) % NX
        py = (qy + k % NY) % NY
        return px * NY + py

    def remote(src, dst, ss, rs, dev):
        return pltpu.make_async_remote_copy(
            src_ref=src, dst_ref=dst, send_sem=ss, recv_sem=rs, device_id=dev, device_id_type=MESH
        )

    loads = []
    for i, (src, dst) in enumerate(
        (
            (act_h.at[0], act_v),
            (grad_h.at[0], grad_v),
            (act_h.at[0, :, pl.ds(pl.multiple_of(f * BLK, BLK), BLK)], acts.at[f]),
            (cot_h.at[0], cot_v),
            (w_h.at[0], w_v),
            (mom_h.at[0], mom_v),
            (par_h.at[0], par_v),
        )
    ):
        cp = pltpu.make_async_copy(src, dst, load_sem.at[i])
        cp.start()
        loads.append(cp)

    barrier = pltpu.get_barrier_semaphore()

    def greet(k, carry):
        pl.semaphore_signal(barrier, inc=1, device_id=(peer(k) * 2 + half, f), device_id_type=MESH)
        return carry

    lax.fori_loop(1, NQ, greet, 0)
    pl.semaphore_signal(barrier, inc=1, device_id=(q * 2 + 1 - half, f), device_id_type=MESH)
    for k in range(1, NF):
        pl.semaphore_signal(barrier, inc=1, device_id=(r, (f + k) % NF), device_id_type=MESH)
    pl.semaphore_wait(barrier, NQ - 1 + 1 + NF - 1)

    loads[0].wait()
    for k in (4, 3, 5, 2, 6, 1, 7):
        to = (f + k) % NF
        remote(
            act_v.at[:, pl.ds(pl.multiple_of(to * BLK, BLK), BLK)], acts.at[f], act_send, act_recv.at[f], (r, to)
        ).start()

    loads[1].wait()
    for s in range(CUTS):

        def leg_one(k, carry, s=s):
            to = peer(k)
            remote(
                grad_v.at[pl.ds(pl.multiple_of(to * ROWS, ROWS), ROWS), pl.ds(s * CW, CW)],
                met[s].at[q], one_send.at[s], one_recv.at[s], (to * 2 + half, f),
            ).start()
            return carry

        lax.fori_loop(1, NQ, leg_one, 0)
        met[s][q] = grad_v[pl.ds(pl.multiple_of(q * ROWS, ROWS), ROWS), pl.ds(s * CW, CW)]

    def square(i, acc):
        a = act_v[:, pl.ds(pl.multiple_of(i * 512, 512), 512)].astype(f32)
        return acc + a * a

    total = lax.fori_loop(0, D // 512, square, jnp.zeros((TOK, 512), f32))
    inv_rms = lax.rsqrt(jnp.sum(total, axis=-1, keepdims=True) * (1.0 / D) + NORM_EPS)
    rms_v[...] = jnp.broadcast_to(inv_rms, (TOK, 128))

    loads[3].wait()
    cots[f] = (cot_v[...].astype(f32) * inv_rms).astype(bf16)

    def cot_up(b):
        return remote(cots.at[b * 2 + c], cots.at[b * 2 + c], cu_send.at[b], c_recv.at[b * 2 + c], at(p + 1, c))

    def cot_down(b):
        return remote(cots.at[b * 2 + c], cots.at[b * 2 + c], cd_send.at[b], c_recv.at[b * 2 + c], at(p - 1, c))

    def cot_across(b):
        return remote(cots.at[b * 2 + c], cots.at[b * 2 + c], cx_send.at[b], c_recv.at[b * 2 + c], at(p, 1 - c))

    @pl.when(p < NP - 1)
    def _():
        cot_up(p).start()

    @pl.when(p > 0)
    def _():
        cot_down(p).start()

    cot_across(p).start()

    gain = gain_v[:, pl.ds(pl.multiple_of(f * BLK, BLK), BLK)]
    gcol[...] = jnp.transpose(jnp.broadcast_to(gain, (128, BLK)))
    loads[4].wait()
    wide_w[...] = (w_v[...].astype(f32) * gcol[:, 0:1]).astype(bf16)

    def z_copy(s):
        return remote(
            met[s].at[pl.ds(0, NQ)], met[s].at[pl.ds(NQ, NQ)], z_send.at[s], z_recv.at[s], (q * 2 + 1 - half, f)
        )

    def all_but_one(ref, ss, rs):
        return remote(ref.at[pl.ds(0, NQ - 1)], ref.at[pl.ds(0, NQ - 1)], ss, rs, (r, f))

    for s in range(CUTS):
        all_but_one(met[s], one_send.at[s], one_recv.at[s]).wait_recv()
        z_copy(s).start()

    for k in range(1, NP):

        @pl.when(p >= k)
        def _(k=k):
            b = p - k
            cot_up(b).wait_recv()
            cot_across(b).start()

            @pl.when(p < NP - 1)
            def _():
                cot_up(b).start()

        @pl.when(p < NP - k)
        def _(k=k):
            b = p + k
            cot_down(b).wait_recv()
            cot_across(b).start()

            @pl.when(p > 0)
            def _():
                cot_down(b).start()

    def act_arrival(b):
        return remote(acts.at[b], acts.at[b], act_send, act_recv.at[b], (r, f))

    def across(j):
        return remote(x_out.at[j], x_in.at[j], x_send.at[j], x_recv.at[j], at(p, 1 - c))

    loads[2].wait()
    for k in range(NP):
        j = (p + k) % NP
        if k > 0:
            act_arrival(j * 2 + c).wait_recv()
        act_arrival(j * 2 + 1 - c).wait_recv()
        x_out[j] = jnp.dot(acts[j * 2 + 1 - c], wide_w[...], preferred_element_type=f32).astype(bf16)
        across(j).start()
        own_part[j] = jnp.dot(acts[j * 2 + c], wide_w[...], preferred_element_type=f32)

    def up(j):
        return remote(u_out.at[j], u_in.at[j], u_send.at[j], u_recv.at[j], at(p + 1, c))

    def down(j):
        return remote(d_out.at[j], d_in.at[j], d_send.at[j], d_recv.at[j], at(p - 1, c))

    for k in range(NP - 1, 0, -1):

        @pl.when(p + k < NP)
        def _(k=k):
            j = p + k
            across(j).wait_recv()

            @pl.when(p > 0)
            def _():
                up(j).wait_recv()
                u_out[j] = (own_part[j] + x_in[j].astype(f32) + u_in[j].astype(f32)).astype(bf16)

            @pl.when(p == 0)
            def _():
                u_out[j] = (own_part[j] + x_in[j].astype(f32)).astype(bf16)

            up(j).start()

        @pl.when(p - k >= 0)
        def _(k=k):
            j = p - k
            across(j).wait_recv()

            @pl.when(p < NP - 1)
            def _():
                down(j).wait_recv()
                d_out[j] = (own_part[j] + x_in[j].astype(f32) + d_in[j].astype(f32)).astype(bf16)

            @pl.when(p == NP - 1)
            def _():
                d_out[j] = (own_part[j] + x_in[j].astype(f32)).astype(bf16)

            down(j).start()

    for k in range(NP):
        across_block = ((p + k) % NP) * 2 + 1 - c
        remote(cots.at[across_block], cots.at[across_block], cx_send.at[0], c_recv.at[across_block], (r, f)).wait_recv()
    wide = 256
    for b in range(BLK // wide):
        lanes = pl.ds(b * wide, wide)
        a = acts[:, :, lanes].reshape(NF * TOK, wide)
        m = lax.dot_general(
            a, cots[...].reshape(NF * TOK, KC), (((0,), (0,)), ((), ())), preferred_element_type=f32
        )
        wgrad_v[lanes, :] = (m * gcol[lanes, 0:1]).astype(bf16)
        prod = m * w_v[lanes, :].astype(f32)
        folded = prod[:, 0:128]
        for e in range(1, KC // 128):
            folded = folded + prod[:, e * 128 : (e + 1) * 128]
        ggrad_v[:, pl.ds(pl.multiple_of(f * BLK + b * wide, wide), wide)] = jnp.sum(
            jnp.transpose(folded), axis=0, keepdims=True
        )
    mine = ggrad_v.at[:, pl.ds(pl.multiple_of(f * BLK, BLK), BLK)]
    for k in range(1, NF):
        remote(mine, mine, g_send, g_recv, (r, (f + k) % NF)).start()
    wgrad_out = pltpu.make_async_copy(wgrad_v, wgrad_h.at[0], out_sem.at[3])
    wgrad_out.start()

    for s in range(CUTS):
        z_copy(s).wait_recv()

        def choose(k, carry, s=s):
            to = peer(k)
            other = partner[to * 2 + half]
            back[s][to] = met[s][lax.rem(other + half, 2) * NQ + lax.div(other, 2)]
            remote(
                back[s].at[to], mirror[s].at[pl.ds(pl.multiple_of(q * ROWS, ROWS), ROWS)],
                two_send.at[s], two_recv.at[s], (to * 2 + half, f),
            ).start()
            return carry

        lax.fori_loop(1, NQ, choose, 0)
        other = partner[r]
        mirror[s][pl.ds(pl.multiple_of(q * ROWS, ROWS), ROWS), :] = met[s][
            lax.rem(other + half, 2) * NQ + lax.div(other, 2)
        ]

    across(p).wait_recv()
    total = own_part[p] + x_in[p].astype(f32)
    own_part[p] = total

    @pl.when(p > 0)
    def _():
        up(p).wait_recv()
        own_part[p] += u_in[p].astype(f32)

    @pl.when(p < NP - 1)
    def _():
        down(p).wait_recv()
        own_part[p] += d_in[p].astype(f32)

    keys_v[...] = (own_part[p] * rms_v[:, 0:1]).astype(bf16)
    keys_out = pltpu.make_async_copy(keys_v, keys_h.at[0], out_sem.at[2])
    keys_out.start()

    loads[5].wait()
    loads[6].wait()
    for s in range(CUTS):
        seen = remote(
            mirror[s].at[pl.ds(0, BLK - ROWS)], mirror[s].at[pl.ds(0, BLK - ROWS)], two_send.at[s], two_recv.at[s], (r, f)
        )
        seen.wait_recv()
        lanes = pl.ds(s * CW, CW)
        mean = (grad_v[:, lanes].astype(f32) + mirror[s][...].astype(f32)) * 0.5
        moment = MOMENT_RATE * mom_v[:, lanes].astype(f32) + mean
        moment_v[:, lanes] = moment.astype(bf16)
        fresh_v[:, lanes] = (
            par_v[:, lanes].astype(f32) - OUTER_RATE * (mean + MOMENT_RATE * moment)
        ).astype(bf16)
    fresh_out = pltpu.make_async_copy(fresh_v, fresh_h.at[0], out_sem.at[0])
    moment_out = pltpu.make_async_copy(moment_v, moment_h.at[0], out_sem.at[1])
    fresh_out.start()
    moment_out.start()

    seven = ggrad_v.at[:, pl.ds(0, D - BLK)]
    remote(seven, seven, g_send, g_recv, (r, f)).wait()
    ggrad_out = pltpu.make_async_copy(ggrad_v, ggrad_h, out_sem.at[4])
    ggrad_out.start()

    remote(acts.at[pl.ds(0, NF - 1)], acts.at[pl.ds(0, NF - 1)], act_send, act_recv.at[0], (r, f)).wait_send()
    for s in range(CUTS):
        all_but_one(met[s], one_send.at[s], one_recv.at[s]).wait_send()
        z_copy(s).wait_send()
        all_but_one(back[s], two_send.at[s], two_recv.at[s]).wait_send()
    for j in range(NP):
        across(j).wait_send()
        cot_across(j).wait_send()

        @pl.when((p >= j) & (p < NP - 1))
        def _(j=j):
            cot_up(j).wait_send()

        @pl.when((p <= j) & (p > 0))
        def _(j=j):
            cot_down(j).wait_send()

        @pl.when(j > p)
        def _(j=j):
            up(j).wait_send()

        @pl.when(j < p)
        def _(j=j):
            down(j).wait_send()

    for cp in (keys_out, wgrad_out, fresh_out, moment_out, ggrad_out):
        cp.wait()


def wrapped(*refs):
    n = 13 + 6
    head, rest = refs[:n], refs[n:]
    met, back, mirror = rest[:CUTS], rest[CUTS : 2 * CUTS], rest[2 * CUTS : 3 * CUTS]
    body_kernel(*head, met, back, mirror, *rest[3 * CUTS :])


def body(partner, pseudo_grad, momentum, outer_params, activations, norm_gain, key_weight, key_cotangent):
    hbm = pl.BlockSpec(memory_space=pl.ANY)
    vmem = pltpu.VMEM
    dma = pltpu.SemaphoreType.DMA
    tok_blocks = lambda n: vmem((n, TOK, KC), bf16)
    scratch = (
        [vmem((BLK, KC), bf16)] * 3
        + [vmem((TOK, D), bf16), vmem((BLK, KC), bf16), vmem((TOK, KC), bf16)]
        + [vmem((2 * NQ, ROWS, CW), bf16)] * CUTS
        + [vmem((NQ, ROWS, CW), bf16)] * CUTS
        + [vmem((BLK, CW), bf16)] * CUTS
        + [tok_blocks(NF), tok_blocks(NF)]
        + [tok_blocks(NP)] * 6
        + [vmem((NP, TOK, KC), f32)]
        + [
            vmem((BLK, KC), bf16),
            vmem((BLK, 128), f32),
            vmem((TOK, KC), bf16),
            vmem((BLK, KC), bf16),
            vmem((1, D), f32),
            vmem((BLK, KC), bf16),
            vmem((BLK, KC), bf16),
            vmem((TOK, 128), f32),
        ]
        + [dma((7,)), dma((5,))]
        + [dma((CUTS,))] * 6
        + [dma, dma((NF,)), dma((NP,)), dma((NP,)), dma((NP,)), dma((NF,))]
        + [dma((NP,))] * 6
        + [dma, dma]
    )
    return pl.pallas_call(
        wrapped,
        out_shape=(
            jax.ShapeDtypeStruct((1, BLK, KC), bf16),
            jax.ShapeDtypeStruct((1, BLK, KC), bf16),
            jax.ShapeDtypeStruct((1, TOK, KC), bf16),
            jax.ShapeDtypeStruct((1, BLK, KC), bf16),
            jax.ShapeDtypeStruct((1, D), f32),
        ),
        in_specs=[
            pl.BlockSpec(memory_space=pltpu.SMEM), hbm, hbm, hbm, hbm,
            pl.BlockSpec(memory_space=pltpu.VMEM), hbm, hbm,
        ],
        out_specs=[hbm] * 5,
        scratch_shapes=scratch,
        compiler_params=pltpu.CompilerParams(
            collective_id=0, has_side_effects=True, vmem_limit_bytes=62 * 2**20
        ),
        name="step",
    )(partner, pseudo_grad, momentum, outer_params, activations, norm_gain, key_weight, key_cotangent)


def solution(mesh):
    sharded = P("replica", "fsdp", None)
    in_specs = (P(), sharded, sharded, sharded, sharded, P("replica", None), sharded, sharded)
    out_specs = (sharded, sharded, sharded, sharded, P("replica", None))
    return jax.shard_map(body, mesh=mesh, in_specs=in_specs, out_specs=out_specs, check_vma=False)
```

```python
import functools

import jax
import jax.numpy as jnp
from jax import lax
from jax.experimental import pallas as pl
from jax.experimental.pallas import tpu as pltpu
from jax.sharding import PartitionSpec as P

MOMENT_RATE = 0.9
OUTER_RATE = 0.7
NORM_EPS = 1e-05

MESH = pl.DeviceIdType.MESH
NX, NY = 4, 8
NQ = NX * NY
REPS = 2 * NQ
NP = 4
NF = 2 * NP
TOK = 128
D = 4096
BLK = D // NF
KC = 512
CUTS = 4
CW = KC // CUTS
ROWS = BLK // NQ

bf16 = jnp.bfloat16
f32 = jnp.float32


def body_kernel(
    cap,
    partner_h, grad_h, mom_h, par_h, act_h, gain_h, w_h, cot_h,
    fresh_h, moment_h, keys_h, wgrad_h, ggrad_h,
    partner, gain_v, grad_v, mom_v, par_v, act_v, w_v, cot_v,
    met, packed, beyond, back, mirror, fresh_v, moment_v,
    acts, cots, x_in, x_out, near_in, near_out, far_out, far_in, own_part,
    wide_w, gcol, keys_v, wgrad_v, ggrad_v, rms_v,
    load_sem, out_sem, one_send, one_recv, z_send, z_recv, two_send, two_recv,
    act_send, act_recv, cu_send, cd_send, cx_send, c_recv,
    x_send, x_recv, n_send, n_recv, f_send, f_recv, g_send, g_recv,
):
    r = lax.axis_index("replica")
    f = lax.axis_index("fsdp")
    q = r // 2
    half = r % 2
    qx, qy = q // NY, q % NY
    p = f // 2
    c = f % 2

    def at(chip, core):
        return (r, chip * 2 + core)

    def peer(k):
        px = (qx + k // NY) % NX
        py = (qy + k % NY) % NY
        return px * NY + py

    def remote(src, dst, ss, rs, dev):
        return pltpu.make_async_remote_copy(
            src_ref=src, dst_ref=dst, send_sem=ss, recv_sem=rs, device_id=dev, device_id_type=MESH
        )

    def rows_of(i):
        return pl.ds(pl.multiple_of(i * ROWS, ROWS), ROWS)

    def block_of(i):
        return pl.ds(pl.multiple_of(i * BLK, BLK), BLK)

    barrier = pltpu.get_barrier_semaphore()
    loads = [
        pltpu.make_async_copy(src, dst, load_sem.at[i])
        for i, (src, dst) in enumerate(
            (
                (act_h.at[0], act_v),
                (cot_h.at[0], cot_v),
                (gain_h, gain_v),
                (w_h.at[0], w_v),
                (grad_h.at[0], grad_v),
                (act_h.at[0, :, block_of(f)], acts.at[f]),
                (partner_h, partner),
                (mom_h.at[0], mom_v),
                (par_h.at[0], par_v),
            )
        )
    ]

    def act_copy(to):
        return remote(act_v.at[:, block_of(to)], acts.at[f], act_send, act_recv.at[f], (r, to))

    def act_arrival(b):
        return remote(acts.at[b], acts.at[b], act_send, act_recv.at[b], (r, f))

    def cot_up(b):
        return remote(cots.at[b * 2 + c], cots.at[b * 2 + c], cu_send.at[b], c_recv.at[b * 2 + c], at(p + 1, c))

    def cot_down(b):
        return remote(cots.at[b * 2 + c], cots.at[b * 2 + c], cd_send.at[b], c_recv.at[b * 2 + c], at(p - 1, c))

    def cot_across(b):
        return remote(cots.at[b * 2 + c], cots.at[b * 2 + c], cx_send.at[b], c_recv.at[b * 2 + c], at(p, 1 - c))

    def cot_arrival(b):
        return remote(cots.at[b], cots.at[b], cx_send.at[0], c_recv.at[b], (r, f))

    def z_copy(s):
        return remote(met[s], beyond[s], z_send.at[s], z_recv.at[s], (q * 2 + 1 - half, f))

    def all_but_one(ref, ss, rs):
        return remote(ref.at[pl.ds(0, NQ - 1)], ref.at[pl.ds(0, NQ - 1)], ss, rs, (r, f))

    def across(j):
        return remote(x_out.at[j], x_in.at[j], x_send.at[j], x_recv.at[j], at(p, 1 - c))

    near_chip = p + 1 - 2 * (p % 2)
    edge, inner = p % 3 == 0, p % 3 > 0
    far_chips = (3 - 3 * (p // 2), 2 - p // 2)

    def near(j):
        return remote(near_out.at[j], near_in.at[j], n_send.at[j], n_recv.at[j], at(near_chip, c))

    def far(j):
        return remote(far_out.at[j], far_in, f_send.at[j], f_recv, at(j, c))

    def load_and_greet():
        for cp in loads:
            cp.start()

        def greet(k, carry):
            pl.semaphore_signal(barrier, inc=1, device_id=(peer(k) * 2 + half, f), device_id_type=MESH)
            return carry

        lax.fori_loop(1, NQ, greet, 0)
        pl.semaphore_signal(barrier, inc=1, device_id=(q * 2 + 1 - half, f), device_id_type=MESH)
        for k in range(1, NF):
            pl.semaphore_signal(barrier, inc=1, device_id=(r, (f + k) % NF), device_id_type=MESH)

    def norm():
        loads[0].wait()

        def square(i, acc):
            a = act_v[:, pl.ds(pl.multiple_of(i * 512, 512), 512)].astype(f32)
            return acc + a * a

        total = lax.fori_loop(0, D // 512, square, jnp.zeros((TOK, 512), f32))
        inv_rms = lax.rsqrt(jnp.sum(total, axis=-1, keepdims=True) * (1.0 / D) + NORM_EPS)
        rms_v[...] = jnp.broadcast_to(inv_rms, (TOK, 128))
        loads[1].wait()
        cots[f] = (cot_v[...].astype(f32) * inv_rms).astype(bf16)
        loads[2].wait()
        gcol[...] = jnp.transpose(jnp.broadcast_to(gain_v[:, block_of(f)], (128, BLK)))
        loads[3].wait()
        wide_w[...] = (w_v[...].astype(f32) * gcol[:, 0:1]).astype(bf16)
        loads[4].wait()

    def leg_one():
        for s in range(CUTS):

            def send(k, carry, s=s):
                to = peer(k)
                remote(
                    grad_v.at[rows_of(to), pl.ds(s * CW, CW)],
                    met[s].at[q], one_send.at[s], one_recv.at[s], (to * 2 + half, f),
                ).start()
                return carry

            lax.fori_loop(1, NQ, send, 0)
            met[s][q] = grad_v[rows_of(q), pl.ds(s * CW, CW)]

    def crossing(i, side):
        return lax.rem(partner[i * 2 + side] + side, 2)

    def tables():
        loads[6].wait()

    def leg_z(s):
        all_but_one(met[s], one_send.at[s], one_recv.at[s]).wait_recv()

        z_copy(s).start()

    def leg_two(s):
        z_copy(s).wait_recv()

        def mirror_of(to):
            other = partner[to * 2 + half]
            i = lax.div(other, 2)
            here = met[s][i]
            there = beyond[s][i]
            return jnp.where(lax.rem(other + half, 2) == 1, there, here)

        def send(k, carry):
            to = peer(k)
            back[s][to] = mirror_of(to)
            remote(
                back[s].at[to], mirror[s].at[rows_of(q)], two_send.at[s], two_recv.at[s], (to * 2 + half, f)
            ).start()
            return carry

        lax.fori_loop(1, NQ, send, 0)
        mirror[s][rows_of(q), :] = mirror_of(q)

    def outer_step(s):
        remote(
            mirror[s].at[pl.ds(0, BLK - ROWS)], mirror[s].at[pl.ds(0, BLK - ROWS)],
            two_send.at[s], two_recv.at[s], (r, f),
        ).wait_recv()
        lanes = pl.ds(s * CW, CW)
        mean = (grad_v[:, lanes].astype(f32) + mirror[s][...].astype(f32)) * 0.5
        moment = MOMENT_RATE * mom_v[:, lanes].astype(f32) + mean
        moment_v[s][...] = moment.astype(bf16)
        fresh_v[s][...] = (
            par_v[:, lanes].astype(f32) - OUTER_RATE * (mean + MOMENT_RATE * moment)
        ).astype(bf16)
        step_out[2 * s].start()
        step_out[2 * s + 1].start()

    def cots_begin():
        @pl.when(p < NP - 1)
        def _():
            cot_up(p).start()

        @pl.when(p > 0)
        def _():
            cot_down(p).start()

        cot_across(p).start()

    def cots_onward(k):
        @pl.when(p >= k)
        def _():
            b = p - k
            cot_up(b).wait_recv()
            cot_across(b).start()

            @pl.when(p < NP - 1)
            def _():
                cot_up(b).start()

        @pl.when(p < NP - k)
        def _():
            b = p + k
            cot_down(b).wait_recv()
            cot_across(b).start()

            @pl.when(p > 0)
            def _():
                cot_down(b).start()

    def partial_keys(j, own):
        if own:
            loads[5].wait()
        else:
            act_arrival(j * 2 + c).wait_recv()
        act_arrival(j * 2 + 1 - c).wait_recv()
        x_out[j] = jnp.dot(acts[j * 2 + 1 - c], wide_w[...], preferred_element_type=f32).astype(bf16)
        across(j).start()
        own_part[j] = jnp.dot(acts[j * 2 + c], wide_w[...], preferred_element_type=f32)

    def sum_near(j):
        across(j).wait_recv()
        near_out[j] = (own_part[j] + x_in[j].astype(f32)).astype(bf16)
        near(j).start()

    def sum_far(j):
        across(j).wait_recv()
        near(j).wait_recv()
        far_out[j] = (own_part[j] + x_in[j].astype(f32) + near_in[j].astype(f32)).astype(bf16)
        far(j).start()

    keys_out = pltpu.make_async_copy(keys_v, keys_h.at[0], out_sem.at[0])
    wgrad_out = pltpu.make_async_copy(wgrad_v, wgrad_h.at[0], out_sem.at[1])
    ggrad_out = pltpu.make_async_copy(ggrad_v, ggrad_h, out_sem.at[2])
    step_out = []
    for s in range(CUTS):
        step_out.append(pltpu.make_async_copy(fresh_v[s], fresh_h.at[s], out_sem.at[3 + s]))
        step_out.append(pltpu.make_async_copy(moment_v[s], moment_h.at[s], out_sem.at[3 + CUTS + s]))

    def finish_keys():
        across(p).wait_recv()
        near(p).wait_recv()
        total = own_part[p] + x_in[p].astype(f32) + near_in[p].astype(f32)
        far(p).wait_recv()
        keys_v[...] = ((total + far_in[...].astype(f32)) * rms_v[:, 0:1]).astype(bf16)
        keys_out.start()

    def weight_grad():
        for k in range(NP):
            cot_arrival(((p + k) % NP) * 2 + 1 - c).wait_recv()
        wide = 256
        for b in range(BLK // wide):
            lanes = pl.ds(b * wide, wide)
            a = acts[:, :, lanes].reshape(NF * TOK, wide)
            m = lax.dot_general(
                a, cots[...].reshape(NF * TOK, KC), (((0,), (0,)), ((), ())), preferred_element_type=f32
            )
            wgrad_v[lanes, :] = (m * gcol[lanes, 0:1]).astype(bf16)
            prod = m * w_v[lanes, :].astype(f32)
            folded = prod[:, 0:128]
            for e in range(1, KC // 128):
                folded = folded + prod[:, e * 128 : (e + 1) * 128]
            ggrad_v[:, pl.ds(pl.multiple_of(f * BLK + b * wide, wide), wide)] = jnp.sum(
                jnp.transpose(folded), axis=0, keepdims=True
            )
        mine = ggrad_v.at[:, block_of(f)]
        for k in range(1, NF):
            remote(mine, mine, g_send, g_recv, (r, (f + k) % NF)).start()
        wgrad_out.start()

    def finish_gain():
        seven = ggrad_v.at[:, pl.ds(0, D - BLK)]
        remote(seven, seven, g_send, g_recv, (r, f)).wait()
        ggrad_out.start()

    def drain():
        remote(acts.at[pl.ds(0, NF - 1)], acts.at[pl.ds(0, NF - 1)], act_send, act_recv.at[0], (r, f)).wait_send()
        for s in range(CUTS):
            all_but_one(met[s], one_send.at[s], one_recv.at[s]).wait_send()
            z_copy(s).wait_send()
            all_but_one(back[s], two_send.at[s], two_recv.at[s]).wait_send()
        for j in range(NP):
            across(j).wait_send()
            cot_across(j).wait_send()

            @pl.when((p >= j) & (p < NP - 1))
            def _(j=j):
                cot_up(j).wait_send()

            @pl.when((p <= j) & (p > 0))
            def _(j=j):
                cot_down(j).wait_send()

        near(near_chip).wait_send()
        for j in far_chips:

            @pl.when(edge)
            def _(j=j):
                near(j).wait_send()

            @pl.when(inner)
            def _(j=j):
                far(j).wait_send()

        for cp in (keys_out, wgrad_out, ggrad_out, *step_out):
            cp.wait()

    scope = jax.named_scope
    with scope("load"):
        load_and_greet()
    with scope("greet"):
        pl.semaphore_wait(barrier, NQ - 1 + 1 + NF - 1)
    with scope("norm"):
        norm()
    with scope("send_acts"):
        cots_begin()
        act_copy(p * 2 + 1 - c).start()
        for chip in (*far_chips, near_chip):
            for core in (c, 1 - c):
                act_copy(chip * 2 + core).start()
    with scope("leg_one"):
        leg_one()
    with scope("tables"):
        tables()
    with scope("cots_1"):
        cots_onward(1)
    with scope("leg_z_0"):
        leg_z(0)
    with scope("leg_z_1"):
        leg_z(1)
    with scope("leg_z_2"):
        leg_z(2)
    with scope("leg_z_3"):
        leg_z(3)
    with scope("wait_loads"):
        loads[7].wait()
        loads[8].wait()
    with scope("leg_two_0"):
        leg_two(0)
    with scope("leg_two_1"):
        leg_two(1)
    with scope("partial_keys_own"):
        partial_keys(p, True)
    with scope("partial_keys_far_1"):
        partial_keys(far_chips[0], False)
    with scope("sum_edge_1"):
        @pl.when(edge)
        def _():
            sum_near(far_chips[0])
    with scope("partial_keys_far_2"):
        partial_keys(far_chips[1], False)
    with scope("sum_edge_2"):
        @pl.when(edge)
        def _():
            sum_near(far_chips[1])
    with scope("cots_2"):
        cots_onward(2)
    with scope("sum_inner_1"):
        @pl.when(inner)
        def _():
            sum_far(far_chips[0])
    with scope("sum_inner_2"):
        @pl.when(inner)
        def _():
            sum_far(far_chips[1])
    with scope("leg_two_2"):
        leg_two(2)
    with scope("partial_keys_near"):
        partial_keys(near_chip, False)
    with scope("sum_near"):
        sum_near(near_chip)
    with scope("leg_two_3"):
        leg_two(3)
    with scope("cots_3"):
        cots_onward(3)
    with scope("weight_grad"):
        weight_grad()
    with scope("outer_step_0"):
        outer_step(0)
    with scope("outer_step_1"):
        outer_step(1)
    with scope("outer_step_2"):
        outer_step(2)
    with scope("finish_keys"):
        finish_keys()
    with scope("outer_step_3"):
        outer_step(3)
    with scope("finish_gain"):
        finish_gain()
    with scope("drain"):
        drain()

def wrapped(cap, *refs):
    n = 13 + 8
    head, rest = refs[:n], refs[n:]
    parts = [rest[i * CUTS : (i + 1) * CUTS] for i in range(7)]
    body_kernel(cap, *head, *parts, *rest[7 * CUTS :])


def hand_over(
    fresh_p, moment_p, keys_h, wgrad_h, ggrad_h, fresh_o, moment_o, keys_o, wgrad_o, ggrad_o,
    fresh_a, moment_a, keys_v, wgrad_v, ggrad_v, fresh_v, moment_v, arrive, leave,
):
    inward = [
        pltpu.make_async_copy(src, dst, arrive.at[i])
        for i, (src, dst) in enumerate(
            ((wgrad_h, wgrad_v), (keys_h, keys_v), (ggrad_h, ggrad_v), (fresh_p, fresh_a), (moment_p, moment_a))
        )
    ]
    outward = [
        pltpu.make_async_copy(src, dst, leave.at[i])
        for i, (src, dst) in enumerate(
            ((wgrad_v, wgrad_o), (keys_v, keys_o), (ggrad_v, ggrad_o), (fresh_v, fresh_o), (moment_v, moment_o))
        )
    ]
    for cp in inward:
        cp.start()
    for i in range(5):
        inward[i].wait()
        if i >= 3:
            parts, whole = ((fresh_a, fresh_v), (moment_a, moment_v))[i - 3]
            for s in range(CUTS):
                whole[0, :, pl.ds(s * CW, CW)] = parts[s]
        outward[i].start()
    for cp in outward:
        cp.wait()


def body(partner, pseudo_grad, momentum, outer_params, activations, norm_gain, key_weight, key_cotangent):
    hbm = pl.BlockSpec(memory_space=pl.ANY)
    vmem = pltpu.VMEM
    dma = pltpu.SemaphoreType.DMA
    tok_blocks = lambda n: vmem((n, TOK, KC), bf16)
    parts = (jax.ShapeDtypeStruct((CUTS, BLK, CW), bf16),) * 2
    results = (
        jax.ShapeDtypeStruct((1, BLK, KC), bf16),
        jax.ShapeDtypeStruct((1, BLK, KC), bf16),
        jax.ShapeDtypeStruct((1, TOK, KC), bf16),
        jax.ShapeDtypeStruct((1, BLK, KC), bf16),
        jax.ShapeDtypeStruct((1, D), f32),
    )

    def step(cap, collective_id):
        scratch = (
            [pltpu.SMEM((REPS,), jnp.int32), vmem((1, D), f32)]
            + [vmem((BLK, KC), bf16)] * 3
            + [vmem((TOK, D), bf16), vmem((BLK, KC), bf16), vmem((TOK, KC), bf16)]
            + [vmem((NQ, ROWS, CW), bf16)] * CUTS
            + [vmem((cap, ROWS, CW), bf16)] * (2 * CUTS)
            + [vmem((NQ, ROWS, CW), bf16)] * CUTS
            + [vmem((BLK, CW), bf16)] * (3 * CUTS)
            + [tok_blocks(NF), tok_blocks(NF)]
            + [tok_blocks(NP)] * 5
            + [vmem((TOK, KC), bf16)]
            + [vmem((NP, TOK, KC), f32)]
            + [
                vmem((BLK, KC), bf16),
                vmem((BLK, 128), f32),
                vmem((TOK, KC), bf16),
                vmem((BLK, KC), bf16),
                vmem((1, D), f32),
                vmem((TOK, 128), f32),
            ]
            + [dma((9,)), dma((3 + 2 * CUTS,))]
            + [dma((CUTS,))] * 6
            + [dma, dma((NF,)), dma((NP,)), dma((NP,)), dma((NP,)), dma((NF,))]
            + [dma((NP,))] * 5
            + [dma, dma, dma]
        )
        return pl.pallas_call(
            functools.partial(wrapped, cap),
            out_shape=parts + results[2:],
            in_specs=[hbm] * 8,
            out_specs=[hbm] * 5,
            scratch_shapes=scratch,
            compiler_params=pltpu.CompilerParams(
                collective_id=collective_id, has_side_effects=True, vmem_limit_bytes=62 * 2**20
            ),
            name=f"step_{cap}",
        )

    done = step(NQ, 0)(
        partner, pseudo_grad, momentum, outer_params, activations, norm_gain, key_weight, key_cotangent
    )
    return pl.pallas_call(
        hand_over,
        out_shape=results,
        in_specs=[hbm] * 5,
        out_specs=[hbm] * 5,
        scratch_shapes=[vmem(a.shape, a.dtype) for a in parts + results[2:] + results[:2]] + [dma((5,)), dma((5,))],
        compiler_params=pltpu.CompilerParams(vmem_limit_bytes=62 * 2**20),
        name="hand_over",
    )(*done)


def solution(mesh):
    sharded = P("replica", "fsdp", None)
    in_specs = (P(), sharded, sharded, sharded, sharded, P("replica", None), sharded, sharded)
    out_specs = (sharded, sharded, sharded, sharded, P("replica", None))
    return jax.shard_map(body, mesh=mesh, in_specs=in_specs, out_specs=out_specs, check_vma=False)
```

```python
import functools

import jax
import jax.numpy as jnp
from jax import lax
from jax.experimental import pallas as pl
from jax.experimental.pallas import tpu as pltpu
from jax.sharding import PartitionSpec as P

MOMENT_RATE = 0.9
OUTER_RATE = 0.7
NORM_EPS = 1e-05

MESH = pl.DeviceIdType.MESH
NX, NY = 4, 8
NQ = NX * NY
REPS = 2 * NQ
FEW = 22
NP = 4
NF = 2 * NP
TOK = 128
D = 4096
BLK = D // NF
KC = 512
CUTS = 4
CW = KC // CUTS
ROWS = BLK // NQ

bf16 = jnp.bfloat16
f32 = jnp.float32


def body_kernel(
    cap,
    partner_h, grad_h, mom_h, par_h, act_h, gain_h, w_h, cot_h,
    fresh_h, moment_h, keys_h, wgrad_h, ggrad_h,
    table, table_v, partner_v, gain_v, grad_v, mom_v, par_v, act_v, w_v, cot_v,
    met, packed, beyond, back, mirror, fresh_v, moment_v,
    acts, cots, x_in, x_out, near_in, near_out, far_out, far_in, own_part,
    wide_w, gcol, keys_v, wgrad_v, ggrad_v, rms_v,
    load_sem, out_sem, one_send, one_recv, z_send, z_recv, two_send, two_recv,
    act_send, act_recv, cu_send, cd_send, cx_send, c_recv,
    x_send, x_recv, n_send, n_recv, f_send, f_recv, g_send, g_recv,
):
    r = lax.axis_index("replica")
    f = lax.axis_index("fsdp")
    q = r // 2
    half = r % 2
    qx, qy = q // NY, q % NY
    p = f // 2
    c = f % 2

    def at(chip, core):
        return (r, chip * 2 + core)

    def peer(k):
        px = (qx + k // NY) % NX
        py = (qy + k % NY) % NY
        return px * NY + py

    def remote(src, dst, ss, rs, dev):
        return pltpu.make_async_remote_copy(
            src_ref=src, dst_ref=dst, send_sem=ss, recv_sem=rs, device_id=dev, device_id_type=MESH
        )

    def rows_of(i):
        return pl.ds(pl.multiple_of(i * ROWS, ROWS), ROWS)

    def block_of(i):
        return pl.ds(pl.multiple_of(i * BLK, BLK), BLK)

    barrier = pltpu.get_barrier_semaphore()
    loads = [
        pltpu.make_async_copy(src, dst, load_sem.at[i])
        for i, (src, dst) in enumerate(
            (
                (act_h.at[0], act_v),
                (cot_h.at[0], cot_v),
                (gain_h, gain_v),
                (w_h.at[0], w_v),
                (grad_h.at[0], grad_v),
                (act_h.at[0, :, block_of(f)], acts.at[f]),
                (partner_h, partner_v),
                (mom_h.at[0], mom_v),
                (par_h.at[0], par_v),
            )
        )
    ]

    def act_copy(to):
        return remote(act_v.at[:, block_of(to)], acts.at[f], act_send, act_recv.at[f], (r, to))

    def act_arrival(b):
        return remote(acts.at[b], acts.at[b], act_send, act_recv.at[b], (r, f))

    def cot_up(b):
        return remote(cots.at[b * 2 + c], cots.at[b * 2 + c], cu_send.at[b], c_recv.at[b * 2 + c], at(p + 1, c))

    def cot_down(b):
        return remote(cots.at[b * 2 + c], cots.at[b * 2 + c], cd_send.at[b], c_recv.at[b * 2 + c], at(p - 1, c))

    def cot_across(b):
        return remote(cots.at[b * 2 + c], cots.at[b * 2 + c], cx_send.at[b], c_recv.at[b * 2 + c], at(p, 1 - c))

    def cot_arrival(b):
        return remote(cots.at[b], cots.at[b], cx_send.at[0], c_recv.at[b], (r, f))

    def z_copy(s):
        return remote(packed[s], beyond[s], z_send.at[s], z_recv.at[s], (q * 2 + 1 - half, f))

    def all_but_one(ref, ss, rs):
        return remote(ref.at[pl.ds(0, NQ - 1)], ref.at[pl.ds(0, NQ - 1)], ss, rs, (r, f))

    def across(j):
        return remote(x_out.at[j], x_in.at[j], x_send.at[j], x_recv.at[j], at(p, 1 - c))

    near_chip = p + 1 - 2 * (p % 2)
    edge, inner = p % 3 == 0, p % 3 > 0
    far_chips = (3 - 3 * (p // 2), 2 - p // 2)

    def near(j):
        return remote(near_out.at[j], near_in.at[j], n_send.at[j], n_recv.at[j], at(near_chip, c))

    def far(j):
        return remote(far_out.at[j], far_in, f_send.at[j], f_recv, at(j, c))

    def load_and_greet():
        for cp in loads:
            cp.start()

        def greet(k, carry):
            pl.semaphore_signal(barrier, inc=1, device_id=(peer(k) * 2 + half, f), device_id_type=MESH)
            return carry

        lax.fori_loop(1, NQ, greet, 0)
        pl.semaphore_signal(barrier, inc=1, device_id=(q * 2 + 1 - half, f), device_id_type=MESH)
        for k in range(1, NF):
            pl.semaphore_signal(barrier, inc=1, device_id=(r, (f + k) % NF), device_id_type=MESH)

    def norm():
        loads[0].wait()

        def square(i, acc):
            a = act_v[:, pl.ds(pl.multiple_of(i * 512, 512), 512)].astype(f32)
            return acc + a * a

        total = lax.fori_loop(0, D // 512, square, jnp.zeros((TOK, 512), f32))
        inv_rms = lax.rsqrt(jnp.sum(total, axis=-1, keepdims=True) * (1.0 / D) + NORM_EPS)
        rms_v[...] = jnp.broadcast_to(inv_rms, (TOK, 128))
        loads[1].wait()
        cot_v[...] = (cot_v[...].astype(f32) * inv_rms).astype(bf16)
        loads[2].wait()
        gcol[...] = jnp.transpose(jnp.broadcast_to(gain_v[:, block_of(f)], (128, BLK)))
        loads[3].wait()
        wide_w[...] = (w_v[...].astype(f32) * gcol[:, 0:1]).astype(bf16)
        loads[4].wait()

    def leg_one():
        for s in range(CUTS):

            def send(k, carry, s=s):
                to = peer(k)
                remote(
                    grad_v.at[rows_of(to), pl.ds(s * CW, CW)],
                    met[s].at[q], one_send.at[s], one_recv.at[s], (to * 2 + half, f),
                ).start()
                return carry

            lax.fori_loop(1, NQ, send, 0)
            met[s][q] = grad_v[rows_of(q), pl.ds(s * CW, CW)]

    def tables():
        loads[6].wait()
        i32 = jnp.int32
        table_v[...] = jnp.zeros((8, 128), i32)
        down = lax.broadcasted_iota(i32, (REPS, REPS), 0)
        along = lax.broadcasted_iota(i32, (REPS, REPS), 1)
        other = jnp.broadcast_to(partner_v[...], (REPS, REPS))
        crosses = (other + along) & 1
        own = jnp.where(down == along, crosses, 0)
        crosses_down = jnp.broadcast_to(jnp.sum(own, axis=1, keepdims=True), (REPS, REPS))
        before = jnp.where((down < other) & (((down + other) & 1) == 0), crosses_down, 0)
        rank_other = jnp.sum(before, axis=0, keepdims=True)
        row = partner_v[...]
        row_crosses = (row + along[0:1, :]) & 1
        table_v[0:1, 0:REPS] = jnp.where(row_crosses == 1, NQ + rank_other, row >> 1)
        ahead = jnp.where((along < down) & (((along + down) & 1) == 0), crosses, 0)
        rank = jnp.broadcast_to(jnp.sum(ahead, axis=1, keepdims=True), (REPS, REPS))
        side, place = along // NQ, along % NQ
        hit = (crosses_down == 1) & ((down & 1) == side) & (rank == place)
        table_v[1:2, 0:REPS] = jnp.sum(jnp.where(hit, down >> 1, 0), axis=0, keepdims=True)
        copy = pltpu.make_async_copy(table_v, table, load_sem.at[9])
        copy.start()
        copy.wait()

    def leg_z(s):
        all_but_one(met[s], one_send.at[s], one_recv.at[s]).wait_recv()

        def pack(j, carry):
            packed[s][j] = met[s][table[1, half * NQ + j]]
            return carry

        lax.fori_loop(0, cap, pack, 0)
        z_copy(s).start()

    def leg_two(s):
        z_copy(s).wait_recv()

        def mirror_of(to):
            i = table[0, to * 2 + half]
            here = met[s][jnp.minimum(i, NQ - 1)]
            there = beyond[s][jnp.clip(i - NQ, 0, cap - 1)]
            return jnp.where(i >= NQ, there, here)

        def send(k, carry):
            to = peer(k)
            back[s][to] = mirror_of(to)
            remote(
                back[s].at[to], mirror[s].at[rows_of(q)], two_send.at[s], two_recv.at[s], (to * 2 + half, f)
            ).start()
            return carry

        lax.fori_loop(1, NQ, send, 0)
        mirror[s][rows_of(q), :] = mirror_of(q)

    def outer_step(s):
        remote(
            mirror[s].at[pl.ds(0, BLK - ROWS)], mirror[s].at[pl.ds(0, BLK - ROWS)],
            two_send.at[s], two_recv.at[s], (r, f),
        ).wait_recv()
        lanes = pl.ds(s * CW, CW)
        mean = (grad_v[:, lanes].astype(f32) + mirror[s][...].astype(f32)) * 0.5
        moment = MOMENT_RATE * mom_v[:, lanes].astype(f32) + mean
        moment_v[s][...] = moment.astype(bf16)
        fresh_v[s][...] = (
            par_v[:, lanes].astype(f32) - OUTER_RATE * (mean + MOMENT_RATE * moment)
        ).astype(bf16)
        step_out[2 * s].start()
        step_out[2 * s + 1].start()

    def cots_begin():
        cots[f] = cot_v[...]

        @pl.when(p < NP - 1)
        def _():
            cot_up(p).start()

        @pl.when(p > 0)
        def _():
            cot_down(p).start()

        cot_across(p).start()

    def cots_onward(k):
        @pl.when(p >= k)
        def _():
            b = p - k
            cot_up(b).wait_recv()
            cot_across(b).start()

            @pl.when(p < NP - 1)
            def _():
                cot_up(b).start()

        @pl.when(p < NP - k)
        def _():
            b = p + k
            cot_down(b).wait_recv()
            cot_across(b).start()

            @pl.when(p > 0)
            def _():
                cot_down(b).start()

    def partial_keys(j, own):
        if own:
            loads[5].wait()
        else:
            act_arrival(j * 2 + c).wait_recv()
        act_arrival(j * 2 + 1 - c).wait_recv()
        x_out[j] = jnp.dot(acts[j * 2 + 1 - c], wide_w[...], preferred_element_type=f32).astype(bf16)
        across(j).start()
        own_part[j] = jnp.dot(acts[j * 2 + c], wide_w[...], preferred_element_type=f32)

    def sum_near(j):
        across(j).wait_recv()
        near_out[j] = (own_part[j] + x_in[j].astype(f32)).astype(bf16)
        near(j).start()

    def sum_far(j):
        across(j).wait_recv()
        near(j).wait_recv()
        far_out[j] = (own_part[j] + x_in[j].astype(f32) + near_in[j].astype(f32)).astype(bf16)
        far(j).start()

    keys_out = pltpu.make_async_copy(keys_v, keys_h.at[0], out_sem.at[0])
    wgrad_out = pltpu.make_async_copy(wgrad_v, wgrad_h.at[0], out_sem.at[1])
    ggrad_out = pltpu.make_async_copy(ggrad_v, ggrad_h, out_sem.at[2])
    step_out = []
    for s in range(CUTS):
        step_out.append(pltpu.make_async_copy(fresh_v[s], fresh_h.at[s], out_sem.at[3 + s]))
        step_out.append(pltpu.make_async_copy(moment_v[s], moment_h.at[s], out_sem.at[3 + CUTS + s]))

    def finish_keys():
        across(p).wait_recv()
        near(p).wait_recv()
        total = own_part[p] + x_in[p].astype(f32) + near_in[p].astype(f32)
        far(p).wait_recv()
        keys_v[...] = ((total + far_in[...].astype(f32)) * rms_v[:, 0:1]).astype(bf16)
        keys_out.start()

    def weight_grad():
        for k in range(NP):
            cot_arrival(((p + k) % NP) * 2 + 1 - c).wait_recv()
        wide = 256
        for b in range(BLK // wide):
            lanes = pl.ds(b * wide, wide)
            a = acts[:, :, lanes].reshape(NF * TOK, wide)
            m = lax.dot_general(
                a, cots[...].reshape(NF * TOK, KC), (((0,), (0,)), ((), ())), preferred_element_type=f32
            )
            wgrad_v[lanes, :] = (m * gcol[lanes, 0:1]).astype(bf16)
            prod = m * w_v[lanes, :].astype(f32)
            folded = prod[:, 0:128]
            for e in range(1, KC // 128):
                folded = folded + prod[:, e * 128 : (e + 1) * 128]
            ggrad_v[:, pl.ds(pl.multiple_of(f * BLK + b * wide, wide), wide)] = jnp.sum(
                jnp.transpose(folded), axis=0, keepdims=True
            )
        mine = ggrad_v.at[:, block_of(f)]
        for k in range(1, NF):
            remote(mine, mine, g_send, g_recv, (r, (f + k) % NF)).start()
        wgrad_out.start()

    def finish_gain():
        seven = ggrad_v.at[:, pl.ds(0, D - BLK)]
        remote(seven, seven, g_send, g_recv, (r, f)).wait()
        ggrad_out.start()

    def drain():
        remote(acts.at[pl.ds(0, NF - 1)], acts.at[pl.ds(0, NF - 1)], act_send, act_recv.at[0], (r, f)).wait_send()
        for s in range(CUTS):
            all_but_one(met[s], one_send.at[s], one_recv.at[s]).wait_send()
            z_copy(s).wait_send()
            all_but_one(back[s], two_send.at[s], two_recv.at[s]).wait_send()
        for j in range(NP):
            across(j).wait_send()
            cot_across(j).wait_send()

            @pl.when((p >= j) & (p < NP - 1))
            def _(j=j):
                cot_up(j).wait_send()

            @pl.when((p <= j) & (p > 0))
            def _(j=j):
                cot_down(j).wait_send()

        near(near_chip).wait_send()
        for j in far_chips:

            @pl.when(edge)
            def _(j=j):
                near(j).wait_send()

            @pl.when(inner)
            def _(j=j):
                far(j).wait_send()

        for cp in (keys_out, wgrad_out, ggrad_out, *step_out):
            cp.wait()

    scope = jax.named_scope
    with scope("load"):
        load_and_greet()
    with scope("norm"):
        norm()
    with scope("greet"):
        pl.semaphore_wait(barrier, NQ - 1 + 1 + NF - 1)
    with scope("send_acts"):
        cots_begin()
        act_copy(p * 2 + 1 - c).start()
        for chip in (*far_chips, near_chip):
            for core in (c, 1 - c):
                act_copy(chip * 2 + core).start()
    with scope("leg_one"):
        leg_one()
    with scope("tables"):
        tables()
    with scope("cots_1"):
        cots_onward(1)
    with scope("leg_z_0"):
        leg_z(0)
    with scope("leg_z_1"):
        leg_z(1)
    with scope("leg_z_2"):
        leg_z(2)
    with scope("leg_z_3"):
        leg_z(3)
    with scope("wait_loads"):
        loads[7].wait()
        loads[8].wait()
    with scope("leg_two_0"):
        leg_two(0)
    with scope("leg_two_1"):
        leg_two(1)
    with scope("partial_keys_own"):
        partial_keys(p, True)
    with scope("partial_keys_far_1"):
        partial_keys(far_chips[0], False)
    with scope("sum_edge_1"):
        @pl.when(edge)
        def _():
            sum_near(far_chips[0])
    with scope("partial_keys_far_2"):
        partial_keys(far_chips[1], False)
    with scope("sum_edge_2"):
        @pl.when(edge)
        def _():
            sum_near(far_chips[1])
    with scope("cots_2"):
        cots_onward(2)
    with scope("sum_inner_1"):
        @pl.when(inner)
        def _():
            sum_far(far_chips[0])
    with scope("sum_inner_2"):
        @pl.when(inner)
        def _():
            sum_far(far_chips[1])
    with scope("leg_two_2"):
        leg_two(2)
    with scope("partial_keys_near"):
        partial_keys(near_chip, False)
    with scope("sum_near"):
        sum_near(near_chip)
    with scope("leg_two_3"):
        leg_two(3)
    with scope("cots_3"):
        cots_onward(3)
    with scope("weight_grad"):
        weight_grad()
    with scope("outer_step_0"):
        outer_step(0)
    with scope("outer_step_1"):
        outer_step(1)
    with scope("outer_step_2"):
        outer_step(2)
    with scope("finish_keys"):
        finish_keys()
    with scope("outer_step_3"):
        outer_step(3)
    with scope("finish_gain"):
        finish_gain()
    with scope("drain"):
        drain()

def wrapped(cap, *refs):
    n = 13 + 10
    head, rest = refs[:n], refs[n:]
    parts = [rest[i * CUTS : (i + 1) * CUTS] for i in range(7)]
    body_kernel(cap, *head, *parts, *rest[7 * CUTS :])


def hand_over(
    fresh_p, moment_p, keys_h, wgrad_h, ggrad_h, fresh_o, moment_o, keys_o, wgrad_o, ggrad_o,
    fresh_a, moment_a, keys_v, wgrad_v, ggrad_v, fresh_v, moment_v, arrive, leave,
):
    inward = [
        pltpu.make_async_copy(src, dst, arrive.at[i])
        for i, (src, dst) in enumerate(
            ((wgrad_h, wgrad_v), (keys_h, keys_v), (ggrad_h, ggrad_v), (fresh_p, fresh_a), (moment_p, moment_a))
        )
    ]
    outward = [
        pltpu.make_async_copy(src, dst, leave.at[i])
        for i, (src, dst) in enumerate(
            ((wgrad_v, wgrad_o), (keys_v, keys_o), (ggrad_v, ggrad_o), (fresh_v, fresh_o), (moment_v, moment_o))
        )
    ]
    for cp in inward:
        cp.start()
    for i in range(5):
        inward[i].wait()
        if i >= 3:
            parts, whole = ((fresh_a, fresh_v), (moment_a, moment_v))[i - 3]
            for s in range(CUTS):
                whole[0, :, pl.ds(s * CW, CW)] = parts[s]
        outward[i].start()
    for cp in outward:
        cp.wait()


def body(partner, pseudo_grad, momentum, outer_params, activations, norm_gain, key_weight, key_cotangent):
    hbm = pl.BlockSpec(memory_space=pl.ANY)
    vmem = pltpu.VMEM
    dma = pltpu.SemaphoreType.DMA
    tok_blocks = lambda n: vmem((n, TOK, KC), bf16)
    parts = (jax.ShapeDtypeStruct((CUTS, BLK, CW), bf16),) * 2
    results = (
        jax.ShapeDtypeStruct((1, BLK, KC), bf16),
        jax.ShapeDtypeStruct((1, BLK, KC), bf16),
        jax.ShapeDtypeStruct((1, TOK, KC), bf16),
        jax.ShapeDtypeStruct((1, BLK, KC), bf16),
        jax.ShapeDtypeStruct((1, D), f32),
    )

    def step(cap, collective_id):
        scratch = (
            [pltpu.SMEM((8, 128), jnp.int32), vmem((8, 128), jnp.int32), vmem((1, REPS), jnp.int32), vmem((1, D), f32)]
            + [vmem((BLK, KC), bf16)] * 3
            + [vmem((TOK, D), bf16), vmem((BLK, KC), bf16), vmem((TOK, KC), bf16)]
            + [vmem((NQ, ROWS, CW), bf16)] * CUTS
            + [vmem((cap, ROWS, CW), bf16)] * (2 * CUTS)
            + [vmem((NQ, ROWS, CW), bf16)] * CUTS
            + [vmem((BLK, CW), bf16)] * (3 * CUTS)
            + [tok_blocks(NF), tok_blocks(NF)]
            + [tok_blocks(NP)] * 5
            + [vmem((TOK, KC), bf16)]
            + [vmem((NP, TOK, KC), f32)]
            + [
                vmem((BLK, KC), bf16),
                vmem((BLK, 128), f32),
                vmem((TOK, KC), bf16),
                vmem((BLK, KC), bf16),
                vmem((1, D), f32),
                vmem((TOK, 128), f32),
            ]
            + [dma((10,)), dma((3 + 2 * CUTS,))]
            + [dma((CUTS,))] * 6
            + [dma, dma((NF,)), dma((NP,)), dma((NP,)), dma((NP,)), dma((NF,))]
            + [dma((NP,))] * 5
            + [dma, dma, dma]
        )
        return pl.pallas_call(
            functools.partial(wrapped, cap),
            out_shape=parts + results[2:],
            in_specs=[hbm] * 8,
            out_specs=[hbm] * 5,
            scratch_shapes=scratch,
            compiler_params=pltpu.CompilerParams(
                collective_id=collective_id, has_side_effects=True, vmem_limit_bytes=62 * 2**20
            ),
            name=f"step_{cap}",
        )

    crossing = jnp.sum(partner.reshape(NQ, 2)[:, 0] % 2)
    done = lax.cond(
        crossing <= FEW, step(FEW, 0), step(NQ, 1),
        partner.reshape(1, REPS), pseudo_grad, momentum, outer_params, activations, norm_gain, key_weight,
        key_cotangent,
    )
    return pl.pallas_call(
        hand_over,
        out_shape=results,
        in_specs=[hbm] * 5,
        out_specs=[hbm] * 5,
        scratch_shapes=[vmem(a.shape, a.dtype) for a in parts + results[2:] + results[:2]] + [dma((5,)), dma((5,))],
        compiler_params=pltpu.CompilerParams(vmem_limit_bytes=62 * 2**20),
        name="hand_over",
    )(*done)


def solution(mesh):
    sharded = P("replica", "fsdp", None)
    in_specs = (P(), sharded, sharded, sharded, sharded, P("replica", None), sharded, sharded)
    out_specs = (sharded, sharded, sharded, sharded, P("replica", None))
    return jax.shard_map(body, mesh=mesh, in_specs=in_specs, out_specs=out_specs, check_vma=False)
```

```python
import functools

import jax
import jax.numpy as jnp
from jax import lax
from jax.experimental import pallas as pl
from jax.experimental.pallas import tpu as pltpu
from jax.sharding import PartitionSpec as P

MOMENT_RATE = 0.9
OUTER_RATE = 0.7
NORM_EPS = 1e-05

MESH = pl.DeviceIdType.MESH
NX, NY = 4, 8
NQ = NX * NY
REPS = 2 * NQ
FEW = 22
NP = 4
NF = 2 * NP
TOK = 128
D = 4096
BLK = D // NF
KC = 512
CUTS = 4
CW = KC // CUTS
ROWS = BLK // NQ

bf16 = jnp.bfloat16
f32 = jnp.float32


def body_kernel(
    cap,
    partner_h, grad_h, mom_h, par_h, act_h, gain_h, w_h, cot_h,
    fresh_h, moment_h, keys_h, wgrad_h, ggrad_h,
    table, table_v, partner_v, gain_v, grad_v, mom_v, par_v, act_v, w_v, cot_v,
    met, packed, beyond, back, mirror, fresh_v, moment_v,
    acts, cots, x_in, x_out, near_in, near_out, far_out, far_in, own_part,
    wide_w, gcol, keys_v, wgrad_v, ggrad_v, rms_v,
    load_sem, out_sem, one_send, one_recv, z_send, z_recv, two_send, two_recv,
    act_send, act_recv, cu_send, cd_send, cx_send, c_recv,
    x_send, x_recv, n_send, n_recv, f_send, f_recv, g_send, g_recv,
):
    r = lax.axis_index("replica")
    f = lax.axis_index("fsdp")
    q = r // 2
    half = r % 2
    qx, qy = q // NY, q % NY
    p = f // 2
    c = f % 2

    def at(chip, core):
        return (r, chip * 2 + core)

    def peer(k):
        px = (qx + k // NY) % NX
        py = (qy + k % NY) % NY
        return px * NY + py

    def remote(src, dst, ss, rs, dev):
        return pltpu.make_async_remote_copy(
            src_ref=src, dst_ref=dst, send_sem=ss, recv_sem=rs, device_id=dev, device_id_type=MESH
        )

    def rows_of(i):
        return pl.ds(pl.multiple_of(i * ROWS, ROWS), ROWS)

    def block_of(i):
        return pl.ds(pl.multiple_of(i * BLK, BLK), BLK)

    barrier = pltpu.get_barrier_semaphore()
    loads = [
        pltpu.make_async_copy(src, dst, load_sem.at[i])
        for i, (src, dst) in enumerate(
            (
                (act_h.at[0], act_v),
                (cot_h.at[0], cot_v),
                (gain_h, gain_v),
                (w_h.at[0], w_v),
                (grad_h.at[0], grad_v),
                (act_h.at[0, :, block_of(f)], acts.at[f]),
                (partner_h, partner_v),
                (mom_h.at[0], mom_v),
                (par_h.at[0], par_v),
            )
        )
    ]

    def act_copy(to):
        return remote(act_v.at[:, block_of(to)], acts.at[f], act_send, act_recv.at[f], (r, to))

    def act_arrival(b):
        return remote(acts.at[b], acts.at[b], act_send, act_recv.at[b], (r, f))

    def cot_up(b):
        return remote(cots.at[b * 2 + c], cots.at[b * 2 + c], cu_send.at[b], c_recv.at[b * 2 + c], at(p + 1, c))

    def cot_down(b):
        return remote(cots.at[b * 2 + c], cots.at[b * 2 + c], cd_send.at[b], c_recv.at[b * 2 + c], at(p - 1, c))

    def cot_across(b):
        return remote(cots.at[b * 2 + c], cots.at[b * 2 + c], cx_send.at[b], c_recv.at[b * 2 + c], at(p, 1 - c))

    def cot_arrival(b):
        return remote(cots.at[b], cots.at[b], cx_send.at[0], c_recv.at[b], (r, f))

    def z_copy(s):
        return remote(packed[s], beyond[s], z_send.at[s], z_recv.at[s], (q * 2 + 1 - half, f))

    def all_but_one(ref, ss, rs):
        return remote(ref.at[pl.ds(0, NQ - 1)], ref.at[pl.ds(0, NQ - 1)], ss, rs, (r, f))

    def across(j):
        return remote(x_out.at[j], x_in.at[j], x_send.at[j], x_recv.at[j], at(p, 1 - c))

    near_chip = p + 1 - 2 * (p % 2)
    edge, inner = p % 3 == 0, p % 3 > 0
    far_chips = (3 - 3 * (p // 2), 2 - p // 2)

    def near(j):
        return remote(near_out.at[j], near_in.at[j], n_send.at[j], n_recv.at[j], at(near_chip, c))

    def far(j):
        return remote(far_out.at[j], far_in, f_send.at[j], f_recv, at(j, c))

    def load_and_greet():
        for cp in loads:
            cp.start()

        def greet(k, carry):
            pl.semaphore_signal(barrier, inc=1, device_id=(peer(k) * 2 + half, f), device_id_type=MESH)
            return carry

        lax.fori_loop(1, NQ, greet, 0)
        pl.semaphore_signal(barrier, inc=1, device_id=(q * 2 + 1 - half, f), device_id_type=MESH)
        for k in range(1, NF):
            pl.semaphore_signal(barrier, inc=1, device_id=(r, (f + k) % NF), device_id_type=MESH)

    def norm():
        loads[0].wait()

        def square(i, acc):
            a = act_v[:, pl.ds(pl.multiple_of(i * 512, 512), 512)].astype(f32)
            return acc + a * a

        total = lax.fori_loop(0, D // 512, square, jnp.zeros((TOK, 512), f32))
        inv_rms = lax.rsqrt(jnp.sum(total, axis=-1, keepdims=True) * (1.0 / D) + NORM_EPS)
        rms_v[...] = jnp.broadcast_to(inv_rms, (TOK, 128))
        loads[1].wait()
        cot_v[...] = (cot_v[...].astype(f32) * inv_rms).astype(bf16)
        loads[2].wait()
        gcol[...] = jnp.transpose(jnp.broadcast_to(gain_v[:, block_of(f)], (128, BLK)))
        loads[3].wait()
        wide_w[...] = (w_v[...].astype(f32) * gcol[:, 0:1]).astype(bf16)
        loads[4].wait()

    def acts_to(chip, core, condition):
        @pl.when(condition)
        def _():
            act_copy(chip * 2 + core).start()

    def leg_one():
        for s in range(CUTS):

            def send(k, carry, s=s):
                to = peer(k)
                remote(
                    grad_v.at[rows_of(to), pl.ds(s * CW, CW)],
                    met[s].at[q], one_send.at[s], one_recv.at[s], (to * 2 + half, f),
                ).start()
                return carry

            lax.fori_loop(1, NQ, send, 0)
            met[s][q] = grad_v[rows_of(q), pl.ds(s * CW, CW)]

    def tables():
        loads[6].wait()
        i32 = jnp.int32
        table_v[...] = jnp.zeros((8, 128), i32)
        down = lax.broadcasted_iota(i32, (REPS, REPS), 0)
        along = lax.broadcasted_iota(i32, (REPS, REPS), 1)
        other = jnp.broadcast_to(partner_v[...], (REPS, REPS))
        crosses = (other + along) & 1
        own = jnp.where(down == along, crosses, 0)
        crosses_down = jnp.broadcast_to(jnp.sum(own, axis=1, keepdims=True), (REPS, REPS))
        before = jnp.where((down < other) & (((down + other) & 1) == 0), crosses_down, 0)
        rank_other = jnp.sum(before, axis=0, keepdims=True)
        row = partner_v[...]
        row_crosses = (row + along[0:1, :]) & 1
        table_v[0:1, 0:REPS] = jnp.where(row_crosses == 1, NQ + rank_other, row >> 1)
        ahead = jnp.where((along < down) & (((along + down) & 1) == 0), crosses, 0)
        rank = jnp.broadcast_to(jnp.sum(ahead, axis=1, keepdims=True), (REPS, REPS))
        side, place = along // NQ, along % NQ
        hit = (crosses_down == 1) & ((down & 1) == side) & (rank == place)
        table_v[1:2, 0:REPS] = jnp.sum(jnp.where(hit, down >> 1, 0), axis=0, keepdims=True)
        copy = pltpu.make_async_copy(table_v, table, load_sem.at[9])
        copy.start()
        copy.wait()

    def leg_z(s):
        all_but_one(met[s], one_send.at[s], one_recv.at[s]).wait_recv()

        def pack(j, carry):
            packed[s][j] = met[s][table[1, half * NQ + j]]
            return carry

        lax.fori_loop(0, cap, pack, 0)
        z_copy(s).start()

    def leg_two(s):
        z_copy(s).wait_recv()

        def mirror_of(to):
            i = table[0, to * 2 + half]
            here = met[s][jnp.minimum(i, NQ - 1)]
            there = beyond[s][jnp.clip(i - NQ, 0, cap - 1)]
            return jnp.where(i >= NQ, there, here)

        def send(k, carry):
            to = peer(k)
            back[s][to] = mirror_of(to)
            remote(
                back[s].at[to], mirror[s].at[rows_of(q)], two_send.at[s], two_recv.at[s], (to * 2 + half, f)
            ).start()
            return carry

        lax.fori_loop(1, NQ, send, 0)
        mirror[s][rows_of(q), :] = mirror_of(q)

    def outer_step(s):
        remote(
            mirror[s].at[pl.ds(0, BLK - ROWS)], mirror[s].at[pl.ds(0, BLK - ROWS)],
            two_send.at[s], two_recv.at[s], (r, f),
        ).wait_recv()
        lanes = pl.ds(s * CW, CW)
        mean = (grad_v[:, lanes].astype(f32) + mirror[s][...].astype(f32)) * 0.5
        moment = MOMENT_RATE * mom_v[:, lanes].astype(f32) + mean
        moment_v[s][...] = moment.astype(bf16)
        fresh_v[s][...] = (
            par_v[:, lanes].astype(f32) - OUTER_RATE * (mean + MOMENT_RATE * moment)
        ).astype(bf16)
        step_out[2 * s].start()
        step_out[2 * s + 1].start()

    def cots_begin():
        cots[f] = cot_v[...]

        @pl.when(p < NP - 1)
        def _():
            cot_up(p).start()

        @pl.when(p > 0)
        def _():
            cot_down(p).start()

        cot_across(p).start()

    def cots_onward(k):
        @pl.when(p >= k)
        def _():
            b = p - k
            cot_arrival(b * 2 + c).wait_recv()
            cot_across(b).start()

            @pl.when(p < NP - 1)
            def _():
                cot_up(b).start()

        @pl.when(p < NP - k)
        def _():
            b = p + k
            cot_arrival(b * 2 + c).wait_recv()
            cot_across(b).start()

            @pl.when(p > 0)
            def _():
                cot_down(b).start()

    def partial_keys(j, own):
        if own:
            loads[5].wait()
        else:
            act_arrival(j * 2 + c).wait_recv()
        act_arrival(j * 2 + 1 - c).wait_recv()
        x_out[j] = jnp.dot(acts[j * 2 + 1 - c], wide_w[...], preferred_element_type=f32).astype(bf16)
        across(j).start()
        own_part[j] = jnp.dot(acts[j * 2 + c], wide_w[...], preferred_element_type=f32)

    def sum_near(j):
        across(j).wait_recv()
        near_out[j] = (own_part[j] + x_in[j].astype(f32)).astype(bf16)
        near(j).start()

    def sum_far(j):
        across(j).wait_recv()
        near(j).wait_recv()
        far_out[j] = (own_part[j] + x_in[j].astype(f32) + near_in[j].astype(f32)).astype(bf16)
        far(j).start()

    keys_out = pltpu.make_async_copy(keys_v, keys_h.at[0], out_sem.at[0])
    wgrad_out = pltpu.make_async_copy(wgrad_v, wgrad_h.at[0], out_sem.at[1])
    ggrad_out = pltpu.make_async_copy(ggrad_v, ggrad_h, out_sem.at[2])
    step_out = []
    for s in range(CUTS):
        step_out.append(pltpu.make_async_copy(fresh_v[s], fresh_h.at[s], out_sem.at[3 + s]))
        step_out.append(pltpu.make_async_copy(moment_v[s], moment_h.at[s], out_sem.at[3 + CUTS + s]))

    def finish_keys():
        across(p).wait_recv()
        near(p).wait_recv()
        total = own_part[p] + x_in[p].astype(f32) + near_in[p].astype(f32)
        far(p).wait_recv()
        keys_v[...] = ((total + far_in[...].astype(f32)) * rms_v[:, 0:1]).astype(bf16)
        keys_out.start()

    def weight_grad():
        for k in range(NP):
            cot_arrival(((p + k) % NP) * 2 + 1 - c).wait_recv()
        wide = 256
        for b in range(BLK // wide):
            lanes = pl.ds(b * wide, wide)
            a = acts[:, :, lanes].reshape(NF * TOK, wide)
            m = lax.dot_general(
                a, cots[...].reshape(NF * TOK, KC), (((0,), (0,)), ((), ())), preferred_element_type=f32
            )
            wgrad_v[lanes, :] = (m * gcol[lanes, 0:1]).astype(bf16)
            prod = m * w_v[lanes, :].astype(f32)
            folded = prod[:, 0:128]
            for e in range(1, KC // 128):
                folded = folded + prod[:, e * 128 : (e + 1) * 128]
            ggrad_v[:, pl.ds(pl.multiple_of(f * BLK + b * wide, wide), wide)] = jnp.sum(
                jnp.transpose(folded), axis=0, keepdims=True
            )
        mine = ggrad_v.at[:, block_of(f)]
        for k in range(1, NF):
            remote(mine, mine, g_send, g_recv, (r, (f + k) % NF)).start()
        wgrad_out.start()

    def finish_gain():
        seven = ggrad_v.at[:, pl.ds(0, D - BLK)]
        remote(seven, seven, g_send, g_recv, (r, f)).wait()
        ggrad_out.start()

    def drain():
        remote(acts.at[pl.ds(0, NF - 1)], acts.at[pl.ds(0, NF - 1)], act_send, act_recv.at[0], (r, f)).wait_send()
        for s in range(CUTS):
            all_but_one(met[s], one_send.at[s], one_recv.at[s]).wait_send()
            z_copy(s).wait_send()
            all_but_one(back[s], two_send.at[s], two_recv.at[s]).wait_send()
        for j in range(NP):
            across(j).wait_send()
            cot_across(j).wait_send()

            @pl.when((p >= j) & (p < NP - 1))
            def _(j=j):
                cot_up(j).wait_send()

            @pl.when((p <= j) & (p > 0))
            def _(j=j):
                cot_down(j).wait_send()

        near(near_chip).wait_send()
        for j in far_chips:

            @pl.when(edge)
            def _(j=j):
                near(j).wait_send()

            @pl.when(inner)
            def _(j=j):
                far(j).wait_send()

        for cp in (keys_out, wgrad_out, ggrad_out, *step_out):
            cp.wait()

    scope = jax.named_scope
    with scope("load"):
        load_and_greet()
    with scope("norm"):
        norm()
    with scope("greet"):
        pl.semaphore_wait(barrier, NQ - 1 + 1 + NF - 1)
    with scope("send_acts"):
        cots_begin()
        act_copy(p * 2 + 1 - c).start()
        acts_to(NP - 1, c, p < NP - 1)
        acts_to(0, c, p > 0)
        acts_to(NP - 1 - p, 1 - c, edge)
        for chip in (lax.rem(p + 2, NP), lax.rem(p + 1 + 2 * (p // 3), NP)):
            for e in (c, 1 - c):
                acts_to(chip, e, edge)
    with scope("leg_one"):
        leg_one()
    with scope("tables"):
        tables()
    with scope("cots_1"):
        cots_onward(1)
        for chip in (NP - 1, 0):
            acts_to(chip, 1 - c, inner)
        for e in (c, 1 - c):
            acts_to(NP - 1 - p, e, inner)
    with scope("leg_z_0"):
        leg_z(0)
    with scope("leg_z_1"):
        leg_z(1)
    with scope("leg_z_2"):
        leg_z(2)
    with scope("leg_z_3"):
        leg_z(3)
    with scope("cots_2"):
        cots_onward(2)
    with scope("wait_loads"):
        loads[7].wait()
        loads[8].wait()
    with scope("leg_two_0"):
        leg_two(0)
    with scope("leg_two_1"):
        leg_two(1)
    with scope("partial_keys_own"):
        partial_keys(p, True)
    with scope("partial_keys_far_1"):
        partial_keys(far_chips[0], False)
    with scope("sum_edge_1"):
        @pl.when(edge)
        def _():
            sum_near(far_chips[0])
    with scope("leg_two_2"):
        leg_two(2)
    with scope("partial_keys_far_2"):
        partial_keys(far_chips[1], False)
    with scope("sum_edge_2"):
        @pl.when(edge)
        def _():
            sum_near(far_chips[1])
    with scope("sum_inner_1"):
        @pl.when(inner)
        def _():
            sum_far(far_chips[0])
    with scope("partial_keys_near"):
        partial_keys(near_chip, False)
    with scope("sum_inner_2"):
        @pl.when(inner)
        def _():
            sum_far(far_chips[1])
    with scope("sum_near"):
        sum_near(near_chip)
    with scope("leg_two_3"):
        leg_two(3)
    with scope("cots_3"):
        cots_onward(3)
    with scope("weight_grad"):
        weight_grad()
    with scope("outer_step_0"):
        outer_step(0)
    with scope("outer_step_1"):
        outer_step(1)
    with scope("outer_step_2"):
        outer_step(2)
    with scope("outer_step_3"):
        outer_step(3)
    with scope("finish_keys"):
        finish_keys()
    with scope("finish_gain"):
        finish_gain()
    with scope("drain"):
        drain()


def wrapped(cap, *refs):
    n = 13 + 10
    head, rest = refs[:n], refs[n:]
    parts = [rest[i * CUTS : (i + 1) * CUTS] for i in range(7)]
    body_kernel(cap, *head, *parts, *rest[7 * CUTS :])


def hand_over(
    fresh_p, moment_p, keys_h, wgrad_h, ggrad_h, fresh_o, moment_o, keys_o, wgrad_o, ggrad_o,
    fresh_a, moment_a, keys_v, wgrad_v, ggrad_v, fresh_v, moment_v, arrive, leave,
):
    inward = [
        pltpu.make_async_copy(src, dst, arrive.at[i])
        for i, (src, dst) in enumerate(
            ((wgrad_h, wgrad_v), (keys_h, keys_v), (ggrad_h, ggrad_v), (fresh_p, fresh_a), (moment_p, moment_a))
        )
    ]
    outward = [
        pltpu.make_async_copy(src, dst, leave.at[i])
        for i, (src, dst) in enumerate(
            ((wgrad_v, wgrad_o), (keys_v, keys_o), (ggrad_v, ggrad_o), (fresh_v, fresh_o), (moment_v, moment_o))
        )
    ]
    for cp in inward:
        cp.start()
    for i in range(5):
        inward[i].wait()
        if i >= 3:
            parts, whole = ((fresh_a, fresh_v), (moment_a, moment_v))[i - 3]
            for s in range(CUTS):
                whole[0, :, pl.ds(s * CW, CW)] = parts[s]
        outward[i].start()
    for cp in outward:
        cp.wait()


def body(partner, pseudo_grad, momentum, outer_params, activations, norm_gain, key_weight, key_cotangent):
    hbm = pl.BlockSpec(memory_space=pl.ANY)
    vmem = pltpu.VMEM
    dma = pltpu.SemaphoreType.DMA
    tok_blocks = lambda n: vmem((n, TOK, KC), bf16)
    parts = (jax.ShapeDtypeStruct((CUTS, BLK, CW), bf16),) * 2
    results = (
        jax.ShapeDtypeStruct((1, BLK, KC), bf16),
        jax.ShapeDtypeStruct((1, BLK, KC), bf16),
        jax.ShapeDtypeStruct((1, TOK, KC), bf16),
        jax.ShapeDtypeStruct((1, BLK, KC), bf16),
        jax.ShapeDtypeStruct((1, D), f32),
    )

    def step(cap, collective_id):
        scratch = (
            [pltpu.SMEM((8, 128), jnp.int32), vmem((8, 128), jnp.int32), vmem((1, REPS), jnp.int32), vmem((1, D), f32)]
            + [vmem((BLK, KC), bf16)] * 3
            + [vmem((TOK, D), bf16), vmem((BLK, KC), bf16), vmem((TOK, KC), bf16)]
            + [vmem((NQ, ROWS, CW), bf16)] * CUTS
            + [vmem((cap, ROWS, CW), bf16)] * (2 * CUTS)
            + [vmem((NQ, ROWS, CW), bf16)] * CUTS
            + [vmem((BLK, CW), bf16)] * (3 * CUTS)
            + [tok_blocks(NF), tok_blocks(NF)]
            + [tok_blocks(NP)] * 5
            + [vmem((TOK, KC), bf16)]
            + [vmem((NP, TOK, KC), f32)]
            + [
                vmem((BLK, KC), bf16),
                vmem((BLK, 128), f32),
                vmem((TOK, KC), bf16),
                vmem((BLK, KC), bf16),
                vmem((1, D), f32),
                vmem((TOK, 128), f32),
            ]
            + [dma((10,)), dma((3 + 2 * CUTS,))]
            + [dma((CUTS,))] * 6
            + [dma, dma((NF,)), dma((NP,)), dma((NP,)), dma((NP,)), dma((NF,))]
            + [dma((NP,))] * 5
            + [dma, dma, dma]
        )
        return pl.pallas_call(
            functools.partial(wrapped, cap),
            out_shape=parts + results[2:],
            in_specs=[hbm] * 8,
            out_specs=[hbm] * 5,
            scratch_shapes=scratch,
            compiler_params=pltpu.CompilerParams(
                collective_id=collective_id, has_side_effects=True, vmem_limit_bytes=62 * 2**20
            ),
            name=f"step_{cap}",
        )

    crossing = jnp.sum(partner.reshape(NQ, 2)[:, 0] % 2)
    done = lax.cond(
        crossing <= FEW, step(FEW, 0), step(NQ, 1),
        partner.reshape(1, REPS), pseudo_grad, momentum, outer_params, activations, norm_gain, key_weight,
        key_cotangent,
    )
    return pl.pallas_call(
        hand_over,
        out_shape=results,
        in_specs=[hbm] * 5,
        out_specs=[hbm] * 5,
        scratch_shapes=[vmem(a.shape, a.dtype) for a in parts + results[2:] + results[:2]] + [dma((5,)), dma((5,))],
        compiler_params=pltpu.CompilerParams(vmem_limit_bytes=62 * 2**20),
        name="hand_over",
    )(*done)


def solution(mesh):
    sharded = P("replica", "fsdp", None)
    in_specs = (P(), sharded, sharded, sharded, sharded, P("replica", None), sharded, sharded)
    out_specs = (sharded, sharded, sharded, sharded, P("replica", None))
    return jax.shard_map(body, mesh=mesh, in_specs=in_specs, out_specs=out_specs, check_vma=False)
```
